32 devices in a mesh: gx: 8 (over z, y), gy: 4 (over x, core).
Axes of the slice: x: 2, y: 2, z: 4, core: 2. Of those that a mesh axis runs over, the one named last changes fastest.
Arguments:
- state: float32 [256, 256, 128], P('gx', 'gy'), may hold values from -6 to 6
- syndromes: int32 [2, 256, 256], P(None, 'gx', 'gy'), may hold values from 0 to 1
- erased: int32 [2, 64, 64], P(None, 'gx', 'gy'), may hold values 0 or 1
- readers: int32 [4096, 1], P(('gx', 'gy')), may hold values from 0 to 31; in each aligned block of 128 rows (0 to 127, 128 to 255, ...) at most 8 rows name the same one
- conv_weight: float32 [9, 128, 128], replicated, may hold values from -0.1875 to 0.1875
- syndrome_table: float32 [2, 128], replicated, may hold values from -6 to 6
- erasure_vector: float32 [128], replicated, may hold values from -6 to 6
- read_weight: float32 [4096, 128], P(('gx', 'gy')), may hold values from -0.5 to 0.5
- erasure_offset: float32 [128], replicated, may hold values from -6 to 6
Outputs:
- final_state: float32 [256, 256, 128], P('gx', 'gy')
The draws below stay inside these ranges and needn't reach their ends.
Inputs may be any that keep to these rules, and one draw needn't show every extreme that they name: `readers`: among the 128 blocks of one device no reader is named more than 8 times, a bound that some block reaches.
All inputs are finite; a program needn't handle non-finite values. No bound on the sum of `erased` on one device may be relied on, other than what follows from the above.
Results may differ from the reference program's by a relative error of at most 0.0003.
Values sent between devices are 32-bit elements; how exact they have to be, the bound alone decides.
A program may use at most 64 MiB of HBM per device.

```python
import math
import jax
import jax.numpy as jnp
import numpy as np
from jax import lax

C = 128
TR = 32
TC = 64
BS = 4
ROUNDS = 2
NR = 256
NC = 256
NBR = 64
NBC = 64
BLK_DEV = 128
CAP = 8
N_GX = 8
N_GY = 4
DEVICES = 32


def with_ends(values, own_key, least, largest):
    extent = values.shape
    index_at = [jax.random.randint(jax.random.fold_in(own_key, axis), (), 0, extent[axis]) for axis in range(len(extent))]
    values = values.at[tuple(index_at)].set(least)
    longest = extent.index(max(extent))
    index_at[longest] = (index_at[longest] + 1) % extent[longest]
    return values.at[tuple(index_at)].set(largest)


def steps_of(stream_key, dims, split, least, high):
    loudness = 1.0
    for axis_at, blocks in split:
        steps = jax.random.uniform(jax.random.fold_in(jax.random.fold_in(stream_key, 6), axis_at), (blocks,), jnp.float32, least / len(split), high / len(split))
        loudness = loudness * jnp.repeat(jnp.exp(steps), dims[axis_at] // blocks).reshape((-1,) + (1,) * (len(dims) - 1 - axis_at))
    return loudness


def shared_out(key, own, number, rows, number_of, top, limit, lean):
    ranking = jax.random.permutation(key, number_of)
    heavy_load, usual = load_shares(number_of, rows * top, limit, lean, True), load_shares(number_of, rows * top, limit, lean, False)
    places = jnp.arange(number_of)

    def named(lengths, offset_by):
        used = int((lengths > 0).sum())
        fixed = max(1, used // 4)
        moved = fixed + (places - fixed + offset_by * (used - fixed)) % max(1, number_of - fixed)
        return jnp.zeros((number_of,), jnp.int32).at[ranking[jnp.where(places < fixed, places, moved)]].set(jnp.asarray(lengths, jnp.int32))

    lengths = jnp.where(number % 4 == 0, named(heavy_load, number // 4), named(usual, number - number // 4 - 1))
    mixed = jax.random.permutation(jax.random.fold_in(own, 3), number_of)
    giver, sink = mixed[0:number_of // 2 * 2:2], mixed[1:number_of // 2 * 2:2]
    slack = jnp.minimum(lengths[giver] - 1, limit - lengths[sink]) // 2
    slack = jnp.where((giver == ranking[0]) | (sink == ranking[0]) | (lengths[sink] == 0), 0, jnp.maximum(slack, 0))
    moved = jax.random.randint(jax.random.fold_in(own, 4), (number_of // 2,), 0, 1 << 20) % (slack + 1)
    lengths = lengths.at[giver].add(-moved).at[sink].add(moved)
    labels = jnp.searchsorted(jnp.cumsum(lengths), jnp.arange(rows * top), side="right").astype(jnp.int32)
    grid = labels.reshape(top, rows).T
    grid = grid[jax.random.permutation(jax.random.fold_in(own, 1), rows)]
    offset_by = jax.random.randint(jax.random.fold_in(own, 2), (rows, 1), 0, top)
    return jnp.take_along_axis(grid, (jnp.arange(top)[None, :] + offset_by) % top, axis=1)


def load_shares(number_of, total, most, lean, full):
    portions = [(1 << 20) // math.isqrt(standing ** lean) + 1 for standing in range(1, number_of + 1)]
    largest = most if full else min(most, max(-(-total // number_of), total * portions[0] // sum(portions)))
    least = 1 if total - largest >= number_of - 1 else 0
    counts, rest = [largest] + [least] * (number_of - 1), total - largest - least * (number_of - 1)
    while rest > 0:
        free = [i for i in range(1, number_of) if counts[i] < largest] or [i for i in range(1, number_of) if counts[i] < most]
        whole, budget = sum([portions[i] for i in free]), rest
        for i in free:
            more = min(most - counts[i], max(1, budget * portions[i] // whole), rest)
            counts[i] = counts[i] + more
            rest = rest - more
    return np.array(counts)


def scatter_about(key, dims, deviation, limit, shards=(), held_as=jnp.bfloat16):
    gain = steps_of(key, dims, shards, -0.22, 0.18) if shards else 1.0
    array = jax.random.normal(key, dims, jnp.float32) * deviation * gain
    return jnp.minimum(jnp.maximum(array, -limit), limit).astype(held_as)


def setup_inputs(seed: int = 0) -> dict:
    streams_of = jax.random.split(jax.random.key(seed), 10)
    state = scatter_about(streams_of[0], (NR, NC, C), 1.0, 6.0, ((0, 8), (1, 4)), jnp.float32)
    syndromes = with_ends(jax.random.randint(streams_of[1], (ROUNDS, NR, NC), 0, 2), jax.random.fold_in(streams_of[1], 1), 0, 1).astype(jnp.int32)
    erased = with_ends((jax.random.randint(streams_of[2], (ROUNDS, NBR, NBC), 0, 4) < 1).astype(jnp.int32), jax.random.fold_in(streams_of[2], 1), 0, 1)
    readers_keys = jax.random.split(jax.random.fold_in(streams_of[3], 1), (DEVICES * BLK_DEV) // BLK_DEV)
    readers_turns = jax.random.permutation(jax.random.fold_in(streams_of[3], 3), (DEVICES * BLK_DEV) // BLK_DEV)
    readers = jax.vmap(lambda own, number: shared_out(jax.random.fold_in(streams_of[3], 2), own, number, BLK_DEV, DEVICES, 1, CAP, 2))(readers_keys, readers_turns).reshape((DEVICES * BLK_DEV, 1))
    conv_weight = scatter_about(streams_of[4], (9, C, C), (9 * C) ** -0.5, 0.1875, (), jnp.float32)
    syndrome_table = scatter_about(streams_of[5], (2, C), 1.0, 6.0, (), jnp.float32)
    erasure_vector = scatter_about(streams_of[6], (C,), 1.0, 6.0, (), jnp.float32)
    read_weight = scatter_about(streams_of[7], (DEVICES * C, C), C ** -0.5, 0.5, ((0, 32),), jnp.float32)
    erasure_offset = scatter_about(streams_of[8], (C,), 1.0, 6.0, (), jnp.float32)
    return {"state": state, "syndromes": syndromes, "erased": erased, "readers": readers, "conv_weight": conv_weight, "syndrome_table": syndrome_table, "erasure_vector": erasure_vector, "read_weight": read_weight, "erasure_offset": erasure_offset}


precise = lax.Precision.HIGHEST


def convolve(field, conv_weight):
    row_count, col_count, channels = field.shape
    padded = jnp.pad(field, ((1, 1), (1, 1), (0, 0)))

    def one_slab(slab_index):
        slab = lax.dynamic_slice_in_dim(padded, slab_index * TR, TR + 2, 0)
        conv_sum = jnp.zeros((TR * col_count, channels), jnp.float32)
        for tap_index in range(9):
            row_off = tap_index // 3
            col_off = tap_index % 3
            shifted = slab[row_off:row_off + TR, col_off:col_off + col_count].reshape(-1, channels)
            conv_sum = conv_sum + jnp.dot(shifted, conv_weight[tap_index], precision=precise, preferred_element_type=jnp.float32)
        return conv_sum.reshape(TR, col_count, channels)

    slabs = lax.map(one_slab, jnp.arange(row_count // TR, dtype=jnp.int32))
    return slabs.reshape(row_count, col_count, channels)


def device_order(values):
    per_rows = TR // BS
    per_cols = TC // BS
    width = values.shape[-1]
    shaped = values.reshape(N_GX, per_rows, N_GY, per_cols, width)
    return shaped.transpose(0, 2, 1, 3, 4).reshape(N_GX * N_GY * per_rows * per_cols, width)


def grid_order(values):
    per_rows = TR // BS
    per_cols = TC // BS
    width = values.shape[-1]
    shaped = values.reshape(N_GX, N_GY, per_rows, per_cols, width)
    return shaped.transpose(0, 2, 1, 3, 4).reshape(NBR, NBC, width)


def spread_cells(values):
    width = values.shape[-1]
    block_grid = values.reshape(NBR, 1, NBC, 1, width)
    return jnp.broadcast_to(block_grid, (NBR, BS, NBC, BS, width)).reshape(NBR * BS, NBC * BS, width)


def reference(state, syndromes, erased, readers, conv_weight, syndrome_table, erasure_vector, read_weight, erasure_offset):
    field = state
    all_weights = read_weight.reshape(DEVICES, C, C)
    reader_rows = readers[:, 0].reshape(DEVICES, BLK_DEV)
    for round_index in range(ROUNDS):
        block_grid = field.reshape(NBR, BS, NBC, BS, C).transpose(0, 2, 1, 3, 4).reshape(NBR, NBC, BS * BS * C)
        block_states = device_order(block_grid).reshape(DEVICES, BLK_DEV, BS * BS * C)
        flag_grid = erased[round_index].astype(jnp.float32)[:, :, None]
        block_flags = device_order(flag_grid).reshape(DEVICES, BLK_DEV, 1)

        def one_device(items):
            states_part, flags_part, readers_part = items
            weights_part = all_weights[readers_part]
            cell_vals = states_part.reshape(BLK_DEV, BS * BS, C)
            mixed_vals = jnp.tanh(jnp.einsum("bpc,bcd->bpd", cell_vals, weights_part, precision=precise))
            return jnp.tanh(jnp.mean(mixed_vals, axis=1) + flags_part * erasure_offset)

        corrections = lax.map(one_device, (block_states, block_flags, reader_rows))
        correction_cells = spread_cells(grid_order(corrections.reshape(DEVICES * BLK_DEV, C)))
        conv_sum = convolve(field, conv_weight)
        erased_cells = spread_cells(erased[round_index][:, :, None])
        bits = syndromes[round_index][:, :, None]
        inputs = jnp.where(erased_cells > 0, erasure_vector, jnp.where(bits == 1, syndrome_table[1], syndrome_table[0]))
        field = 0.5 * field + jnp.tanh(conv_sum + inputs + correction_cells)
    return field
```

```python
import functools

import jax
import jax.numpy as jnp
from jax import lax
from jax.experimental import pallas as pl
from jax.experimental.pallas import tpu as pltpu
from jax.sharding import PartitionSpec as P

MESH = pl.DeviceIdType.MESH
BS = 4
ROUNDS = 2
SLOTS = 8
LEFT = 8
ORDERS = (("z", "y", "x", 0, 64), ("z", "x", "y", 64, 128))
SIDES = ((-1, 0), (1, 0), (0, -1), (0, 1), (-1, -1), (-1, 1), (1, -1), (1, 1))
F32 = jnp.float32
BF16 = jnp.bfloat16


def split_2(values):
    high = values.astype(BF16)
    return high, (values - high.astype(F32)).astype(BF16)


def split_3(values):
    high, rest = values.astype(BF16).astype(F32), values
    rest = rest - high
    mid = rest.astype(BF16).astype(F32)
    return high, mid, rest - mid


def kernel(
    sizes,
    state_ref,
    syn_ref,
    er_ref,
    readers_ref,
    conv_ref,
    table_ref,
    vector_ref,
    read_ref,
    offset_ref,
    out_ref,
    weights,
    padded,
    taps_high,
    taps_low,
    conv_both,
    conv_sum,
    cells,
    sorted_cells,
    pooled,
    pick,
    place,
    spread,
    row_out,
    col_out,
    row_in,
    col_in,
    corner_out,
    corner_in,
    send_sem,
    recv_sem,
    core_send,
    core_recv,
    halo_send,
    halo_recv,
):
    nz, ny, nx = sizes
    lengths = {"z": nz, "y": ny, "x": nx}
    rows, cols, chan = state_ref.shape
    block_rows, block_cols = rows // BS, cols // BS
    blocks = block_rows * block_cols
    slots = nz * ny * nx * 2 * SLOTS
    gx, gy = lax.axis_index("gx"), lax.axis_index("gy")
    at = {"z": gx // ny, "y": gx % ny, "x": gy // 2}
    core = gy % 2
    gx_count, gy_count = nz * ny, nx * 2

    def device(place_of, c):
        return (place_of["z"] * ny + place_of["y"], place_of["x"] * 2 + c)

    def held(order, wave, place_of, c):
        full = order[:wave]
        idx = [pl.ds(0, lengths[d]) if d in full else place_of[d] for d in "zyx"]
        return weights.at[idx[0], idx[1], idx[2], c, pl.ds(order[3], order[4] - order[3]), :]

    def shifted(dim, k):
        moved = dict(at)
        moved[dim] = (at[dim] + k + lengths[dim]) % lengths[dim]
        return moved

    def wave_copies(wave):
        made = []
        n = 0
        for order in ORDERS:
            dim = order[wave]
            for k in range(1, lengths[dim]):
                other, source = shifted(dim, k), shifted(dim, -k)
                mine, theirs = held(order, wave, at, core), held(order, wave, source, core)
                passed = held(order, wave, source, 1 - core)
                out = pltpu.make_async_remote_copy(
                    mine, mine, send_sem.at[wave, n], recv_sem.at[wave, n],
                    device_id=device(other, core), device_id_type=MESH)
                arriving = pltpu.make_async_remote_copy(
                    theirs, theirs, send_sem.at[wave, n], recv_sem.at[wave, n],
                    device_id=device(other, core), device_id_type=MESH)
                on = pltpu.make_async_remote_copy(
                    theirs, theirs, core_send.at[wave, n], core_recv.at[wave, n],
                    device_id=device(at, 1 - core), device_id_type=MESH)
                back = pltpu.make_async_remote_copy(
                    passed, passed, core_send.at[wave, n], core_recv.at[wave, n],
                    device_id=device(at, 1 - core), device_id_type=MESH)
                made.append((out, arriving, on, back))
                n += 1
        return made

    def own_pair():
        made = []
        for c in (core, 1 - core):
            part = weights.at[at["z"], at["y"], at["x"], c]
            made.append(pltpu.make_async_remote_copy(
                part, part, core_send.at[3, 0], core_recv.at[3, 0],
                device_id=device(at, 1 - core), device_id_type=MESH))
        return made

    waves = [wave_copies(w) for w in range(3)]
    own_out, own_in = own_pair()

    there = []
    for dr, dc in SIDES:
        ok = jnp.bool_(True)
        if dr:
            ok = (gx + dr >= 0) & (gx + dr < gx_count)
        if dc:
            more = (gy + dc >= 0) & (gy + dc < gy_count)
            ok = more if not dr else ok & more
        there.append(ok)

    def halo_refs(r, side):
        dr, dc = SIDES[side]
        if side < 2:
            return row_out.at[r, side], row_in.at[r, side]
        if side < 4:
            return col_out.at[r, side - 2], col_in.at[r, side - 2]
        return corner_out.at[r, side - 4], corner_in.at[r, side - 4]

    opposite = (1, 0, 3, 2, 7, 6, 5, 4)

    def halo_copy(r, side):
        dr, dc = SIDES[side]
        src, _ = halo_refs(r, side)
        _, dst = halo_refs(r, opposite[side])
        return pltpu.make_async_remote_copy(
            src, dst, halo_send.at[r, side], halo_recv.at[r, opposite[side]],
            device_id=(gx + dr, gy + dc), device_id_type=MESH)

    def halo_arrival(r, side):
        dr, dc = SIDES[side]
        _, dst = halo_refs(r, side)
        return pltpu.make_async_remote_copy(
            dst, dst, halo_send.at[r, side], halo_recv.at[r, side],
            device_id=(gx + dr, gy + dc), device_id_type=MESH)

    def for_sides(do):
        for side in range(8):
            pl.when(there[side])(functools.partial(do, side))

    def pack_borders(r):
        row_out[r, 0] = padded[1, LEFT:LEFT + cols, :]
        row_out[r, 1] = padded[rows, LEFT:LEFT + cols, :]

        def one(i, _):
            col_out[r, 0, pl.ds(i, 1), :] = padded[1 + i, LEFT:LEFT + 1, :]
            col_out[r, 1, pl.ds(i, 1), :] = padded[1 + i, LEFT + cols - 1:LEFT + cols, :]
            return 0

        lax.fori_loop(0, rows, one, 0, unroll=4)
        for n, (dr, dc) in enumerate(SIDES[4:]):
            line = 1 if dr < 0 else rows
            col = LEFT if dc < 0 else LEFT + cols - 1
            corner_out[r, n] = jnp.broadcast_to(padded[line, col:col + 1, :], (8, chan))

    def place_borders(r):
        padded[0, LEFT:LEFT + cols, :] = row_in[r, 0]
        padded[rows + 1, LEFT:LEFT + cols, :] = row_in[r, 1]

        def one(i, _):
            padded[1 + i, LEFT - 1:LEFT, :] = col_in[r, 0, pl.ds(i, 1), :]
            padded[1 + i, LEFT + cols:LEFT + cols + 1, :] = col_in[r, 1, pl.ds(i, 1), :]
            return 0

        lax.fori_loop(0, rows, one, 0, unroll=4)
        for n, (dr, dc) in enumerate(SIDES[4:]):
            line = 0 if dr < 0 else rows + 1
            col = LEFT - 1 if dc < 0 else LEFT + cols
            padded[line, col:col + 1, :] = corner_in[r, n, 0:1, :]

    weights[at["z"], at["y"], at["x"], core] = read_ref[...]

    def fill(i, _):
        padded[1 + i, LEFT:LEFT + cols, :] = state_ref[i]
        return 0

    lax.fori_loop(0, rows, fill, 0, unroll=2)
    pack_borders(0)

    def clear(side):
        for r in range(ROUNDS):
            _, dst = halo_refs(r, side)
            dst[...] = jnp.zeros(dst.shape, F32)

    for side in range(8):
        pl.when(jnp.logical_not(there[side]))(functools.partial(clear, side))

    barrier = pltpu.get_barrier_semaphore()
    count = jnp.int32(1)
    pl.semaphore_signal(barrier, inc=1, device_id=device(at, 1 - core), device_id_type=MESH)
    for dim in "zyx":
        for k in range(1, lengths[dim]):
            pl.semaphore_signal(barrier, inc=1, device_id=device(shifted(dim, k), core), device_id_type=MESH)
            count = count + 1

    def greet(side):
        dr, dc = SIDES[side]
        pl.semaphore_signal(barrier, inc=1, device_id=(gx + dr, gy + dc), device_id_type=MESH)

    for_sides(greet)
    for side in range(8):
        count = count + there[side].astype(jnp.int32)
    pl.semaphore_wait(barrier, count)

    for out, _, _, _ in waves[0]:
        out.start()
    own_out.start()
    for_sides(lambda side: halo_copy(0, side).start())

    def next_wave(wave):
        for _, arriving, _, _ in waves[wave]:
            arriving.wait_recv()
        if wave + 1 < 3:
            for out, _, _, _ in waves[wave + 1]:
                out.start()
        for _, _, on, _ in waves[wave]:
            on.start()

    first = lax.broadcasted_iota(jnp.int32, (blocks, blocks), 0)
    second = lax.broadcasted_iota(jnp.int32, (blocks, blocks), 1)
    down = jnp.broadcast_to(readers_ref[...].astype(F32), (blocks, blocks))
    across = jnp.sum(jnp.where(first == second, down, 0.0), axis=0, keepdims=True)
    same = jnp.where(down == across, 1.0, 0.0)
    slot_across = SLOTS * across + jnp.sum(jnp.where(first < second, same, 0.0), axis=0, keepdims=True)
    slot_down = SLOTS * down[:, 0:1] + jnp.sum(jnp.where(second < first, same, 0.0), axis=1, keepdims=True)
    slot_at = lax.broadcasted_iota(jnp.int32, (slots, blocks), 0).astype(F32)
    pick[...] = jnp.where(slot_at == slot_across, 1.0, 0.0).astype(BF16)
    slot_at = lax.broadcasted_iota(jnp.int32, (blocks, slots), 1).astype(F32)
    place[...] = jnp.where(slot_at == slot_down, 1.0, 0.0).astype(BF16)

    line = lax.broadcasted_iota(jnp.int32, (16, chan), 0)
    embed = jnp.zeros((16, chan), F32)
    for n, row in enumerate((vector_ref[...], table_ref[1:2, :], table_ref[0:1, :])):
        for m, part in enumerate(split_3(row)):
            embed = jnp.where(line == 3 * n + m, part, embed)
    embed = embed.astype(BF16)
    feature = lax.broadcasted_iota(jnp.int32, (16, cols), 0)

    def split_conv(t, _):
        high, low = split_2(conv_ref[t])
        conv_both[pl.ds(t * chan, chan), 0:chan] = high
        conv_both[pl.ds(t * chan, chan), chan:2 * chan] = low
        return 0

    lax.fori_loop(0, 9, split_conv, 0)

    def build_cells():
        def one(b, _):
            for i in range(BS):
                for q in range(BS):
                    high, low = split_2(padded[1 + BS * b + i, pl.ds(LEFT + q, block_cols, stride=BS), :])
                    cells[i * BS + q, pl.ds(b * block_cols, block_cols), 0:chan] = high
                    cells[i * BS + q, pl.ds(b * block_cols, block_cols), chan:2 * chan] = low
            return 0

        lax.fori_loop(0, block_rows, one, 0)

        def sort(p, _):
            sorted_cells[p] = jnp.dot(pick[...], cells[p], preferred_element_type=F32)
            return 0

        lax.fori_loop(0, BS * BS, sort, 0)

    def build_taps():
        def one(i, _):
            for s in range(3):
                high, low = split_2(padded[i, LEFT - 1 + s:LEFT - 1 + s + cols, :])
                taps_high[i, :, s * chan:(s + 1) * chan] = high
                taps_low[i, :, s * chan:(s + 1) * chan] = low
            return 0

        lax.fori_loop(0, rows + 2, one, 0, unroll=2)

    def convolve():
        step = 8

        def one(n, _):
            def lines(ref):
                parts = [ref[pl.ds(n * step + a, step)].reshape(step * cols, 3 * chan) for a in range(3)]
                return jnp.concatenate(parts, axis=1)

            both = jnp.dot(lines(taps_high), conv_both[...], preferred_element_type=F32)
            low = jnp.dot(lines(taps_low), conv_both[:, 0:chan], preferred_element_type=F32)
            total = both[:, 0:chan] + (both[:, chan:] + low)
            conv_sum[pl.ds(n * step, step)] = total.reshape(step, cols, chan)
            return 0

        lax.fori_loop(0, rows // step, one, 0)

    def read_out(r):
        def one(k, _):
            c, x = k % 2, k // 2 % nx
            z, y = k // (2 * nx * ny), k // (2 * nx) % ny
            high, low = split_2(weights[z, y, x, c])
            side = jnp.concatenate([high, low], axis=1)
            weight = jnp.concatenate([side, side], axis=0)
            vals = sorted_cells[:, pl.ds(pl.multiple_of(k * SLOTS, SLOTS), SLOTS), :]
            vals = vals.reshape(BS * BS * SLOTS, 2 * chan).astype(BF16)
            both = jnp.dot(vals, weight, preferred_element_type=F32)
            mixed = jnp.tanh(both[:, 0:chan] + both[:, chan:])
            mean = jnp.sum(mixed.reshape(BS * BS, SLOTS, chan), axis=0) * (1.0 / (BS * BS))
            pooled[pl.ds(pl.multiple_of(k * SLOTS, SLOTS), SLOTS), :] = mean
            return 0

        lax.fori_loop(0, nz * ny * nx * 2, one, 0, unroll=4)
        high, low = split_2(pooled[...])
        both = jnp.dot(place[...], jnp.concatenate([high, low], axis=1), preferred_element_type=F32)
        mean = both[:, 0:chan] + both[:, chan:]
        lane = lax.broadcasted_iota(jnp.int32, (block_cols, block_cols), 1)
        deep = lax.broadcasted_iota(jnp.int32, (block_cols, block_cols), 0)
        flags = er_ref[r].astype(F32)
        for b in range(block_rows):
            flag = jnp.sum(jnp.where(lane == deep, flags[b:b + 1, :], 0.0), axis=1, keepdims=True)
            part = jnp.tanh(mean[b * block_cols:(b + 1) * block_cols] + flag * offset_ref[...])
            for q in range(BS):
                spread[b, pl.ds(q, block_cols, stride=BS), :] = part

    def combine(r, last):
        wide = jnp.where(
            lax.broadcasted_iota(jnp.int32, (block_cols, cols), 1) // BS
            == lax.broadcasted_iota(jnp.int32, (block_cols, cols), 0), 1.0, 0.0).astype(BF16)
        flag_lanes = jnp.dot(er_ref[r].astype(F32).astype(BF16), wide, preferred_element_type=F32)
        bits_all = syn_ref[r].astype(F32)
        for b in range(block_rows):
            gone = flag_lanes[b:b + 1, :]
            for i in range(b * BS, (b + 1) * BS):
                bits = bits_all[i:i + 1, :]
                one_hot = jnp.where(
                    feature < 3, gone,
                    jnp.where(feature < 6, (1.0 - gone) * bits, (1.0 - gone) * (1.0 - bits))).astype(BF16)
                inputs = lax.dot_general(
                    one_hot, embed, (((0,), (0,)), ((), ())), preferred_element_type=F32)
                old = padded[1 + i, LEFT:LEFT + cols, :]
                new = 0.5 * old + jnp.tanh(conv_sum[i] + inputs + spread[b])
                if last:
                    out_ref[i] = new
                else:
                    padded[1 + i, LEFT:LEFT + cols, :] = new

    build_cells()
    for_sides(lambda side: halo_arrival(0, side).wait_recv())
    place_borders(0)
    build_taps()
    next_wave(0)
    convolve()
    next_wave(1)
    next_wave(2)
    for wave in range(3):
        for _, _, _, back in waves[wave]:
            back.wait_recv()
    own_in.wait_recv()
    read_out(0)
    combine(0, False)
    pack_borders(1)
    for_sides(lambda side: halo_copy(1, side).start())
    build_cells()
    read_out(1)
    for_sides(lambda side: halo_arrival(1, side).wait_recv())
    place_borders(1)
    build_taps()
    convolve()
    combine(1, True)

    for wave in range(3):
        for out, _, on, _ in waves[wave]:
            out.wait_send()
            on.wait_send()
    own_out.wait_send()
    for r in range(ROUNDS):
        for_sides(lambda side: halo_copy(r, side).wait_send())


def solution(mesh):
    gx_count, gy_count = mesh.shape["gx"], mesh.shape["gy"]
    nx = gy_count // 2
    ny = nx
    nz = gx_count // ny
    copies = 2 * max(nz - 1, ny - 1, nx - 1)

    def per_device(state, syndromes, erased, readers, conv, table, vector, read, offset):
        rows, cols, chan = state.shape
        blocks = readers.shape[0]
        slots = gx_count * gy_count * SLOTS
        vmem = pltpu.VMEM
        dma = pltpu.SemaphoreType.DMA
        return pl.pallas_call(
            functools.partial(kernel, (nz, ny, nx)),
            out_shape=jax.ShapeDtypeStruct(state.shape, F32),
            in_specs=[pl.BlockSpec(memory_space=vmem)] * 9,
            out_specs=pl.BlockSpec(memory_space=vmem),
            scratch_shapes=[
                vmem((nz, ny, nx, 2, chan, chan), F32),
                vmem((rows + 2, cols + 16, chan), F32),
                vmem((rows + 2, cols, 3 * chan), BF16),
                vmem((rows + 2, cols, 3 * chan), BF16),
                vmem((9 * chan, 2 * chan), BF16),
                vmem((rows, cols, chan), F32),
                vmem((BS * BS, blocks, 2 * chan), BF16),
                vmem((BS * BS, slots, 2 * chan), F32),
                vmem((slots, chan), F32),
                vmem((slots, blocks), BF16),
                vmem((blocks, slots), BF16),
                vmem((rows // BS, cols, chan), F32),
                vmem((ROUNDS, 2, cols, chan), F32),
                vmem((ROUNDS, 2, rows, chan), F32),
                vmem((ROUNDS, 2, cols, chan), F32),
                vmem((ROUNDS, 2, rows, chan), F32),
                vmem((ROUNDS, 4, 8, chan), F32),
                vmem((ROUNDS, 4, 8, chan), F32),
                dma((3, copies)),
                dma((3, copies)),
                dma((4, copies)),
                dma((4, copies)),
                dma((ROUNDS, 8)),
                dma((ROUNDS, 8)),
            ],
            compiler_params=pltpu.CompilerParams(
                collective_id=0, has_side_effects=True, vmem_limit_bytes=56 * 2**20
            ),
        )(state, syndromes, erased, readers, conv, table, vector.reshape(1, -1), read, offset.reshape(1, -1))

    placed = (
        P("gx", "gy", None),
        P(None, "gx", "gy"),
        P(None, "gx", "gy"),
        P(("gx", "gy"), None),
        P(),
        P(),
        P(),
        P(("gx", "gy"), None),
        P(),
    )
    return jax.shard_map(
        per_device, mesh=mesh, in_specs=placed, out_specs=P("gx", "gy", None), check_vma=False
    )
```

```python
import functools

import jax
import jax.numpy as jnp
from jax import lax
from jax.experimental import pallas as pl
from jax.experimental.pallas import tpu as pltpu
from jax.sharding import PartitionSpec as P

MESH = pl.DeviceIdType.MESH
BS = 4
ROUNDS = 2
SLOTS = 8
LEFT = 8
ORDERS = (
    ("z", "y", "x", 0, 40),
    ("z", "x", "y", 40, 80),
    ("x", "z", "y", 80, 104),
    ("y", "z", "x", 104, 128),
)
STEP = 8
SIDES = ((-1, 0), (1, 0), (0, -1), (0, 1), (-1, -1), (-1, 1), (1, -1), (1, 1))
F32 = jnp.float32
BF16 = jnp.bfloat16


def split_2(values):
    high = values.astype(BF16)
    return high, (values - high.astype(F32)).astype(BF16)


def split_3(values):
    high, rest = values.astype(BF16).astype(F32), values
    rest = rest - high
    mid = rest.astype(BF16).astype(F32)
    return high, mid, rest - mid


def kernel(
    sizes,
    state_ref,
    syn_ref,
    er_ref,
    readers_ref,
    conv_ref,
    table_ref,
    vector_ref,
    read_ref,
    offset_ref,
    out_ref,
    weights,
    padded,
    taps_high,
    taps_low,
    conv_both,
    conv_sum,
    cells,
    sorted_cells,
    pooled,
    pick,
    place,
    spread,
    row_out,
    col_out,
    row_in,
    col_in,
    corner_out,
    corner_in,
    conv_whole,
    inputs,
    local_sem,
    send_sem,
    recv_sem,
    core_send,
    core_recv,
    halo_send,
    halo_recv,
):
    nz, ny, nx = sizes
    lengths = {"z": nz, "y": ny, "x": nx}
    rows, cols, chan = conv_sum.shape
    block_rows, block_cols = rows // BS, cols // BS
    blocks = block_rows * block_cols
    slots = nz * ny * nx * 2 * SLOTS
    gx, gy = lax.axis_index("gx"), lax.axis_index("gy")
    at = {"z": gx // ny, "y": gx % ny, "x": gy // 2}
    core = gy % 2
    gx_count, gy_count = nz * ny, nx * 2

    def device(place_of, c):
        return (place_of["z"] * ny + place_of["y"], place_of["x"] * 2 + c)

    def held(order, wave, place_of, c):
        full = order[:wave]
        idx = [pl.ds(0, lengths[d]) if d in full else place_of[d] for d in "zyx"]
        return weights.at[idx[0], idx[1], idx[2], c, pl.ds(order[3], order[4] - order[3]), :]

    def shifted(dim, k):
        moved = dict(at)
        moved[dim] = (at[dim] + k + lengths[dim]) % lengths[dim]
        return moved

    def wave_copies(o, wave):
        made = []
        order = ORDERS[o]
        dim = order[wave]
        for k in range(1, lengths[dim]):
            other, source = shifted(dim, k), shifted(dim, -k)
            mine, theirs = held(order, wave, at, core), held(order, wave, source, core)
            passed = held(order, wave, source, 1 - core)
            made.append(tuple(
                pltpu.make_async_remote_copy(
                    part, part, sems[0].at[wave, o, k - 1], sems[1].at[wave, o, k - 1],
                    device_id=target, device_id_type=MESH)
                for part, sems, target in (
                    (mine, (send_sem, recv_sem), device(other, core)),
                    (theirs, (send_sem, recv_sem), device(other, core)),
                    (theirs, (core_send, core_recv), device(at, 1 - core)),
                    (passed, (core_send, core_recv), device(at, 1 - core)),
                )))
        return made

    def own_pair():
        made = []
        for c in (core, 1 - core):
            part = weights.at[at["z"], at["y"], at["x"], c]
            made.append(pltpu.make_async_remote_copy(
                part, part, core_send.at[3, 0, 0], core_recv.at[3, 0, 0],
                device_id=device(at, 1 - core), device_id_type=MESH))
        return made

    waves = [[wave_copies(o, w) for w in range(3)] for o in range(len(ORDERS))]
    own_out, own_in = own_pair()

    there = []
    for dr, dc in SIDES:
        ok = jnp.bool_(True)
        if dr:
            ok = (gx + dr >= 0) & (gx + dr < gx_count)
        if dc:
            more = (gy + dc >= 0) & (gy + dc < gy_count)
            ok = more if not dr else ok & more
        there.append(ok)

    def halo_refs(r, side):
        dr, dc = SIDES[side]
        if side < 2:
            return row_out.at[r, side], row_in.at[r, side]
        if side < 4:
            return col_out.at[r, side - 2], col_in.at[r, side - 2]
        return corner_out.at[r, side - 4], corner_in.at[r, side - 4]

    opposite = (1, 0, 3, 2, 7, 6, 5, 4)

    def halo_copy(r, side):
        dr, dc = SIDES[side]
        src, _ = halo_refs(r, side)
        _, dst = halo_refs(r, opposite[side])
        return pltpu.make_async_remote_copy(
            src, dst, halo_send.at[r, side], halo_recv.at[r, opposite[side]],
            device_id=(gx + dr, gy + dc), device_id_type=MESH)

    def halo_arrival(r, side):
        dr, dc = SIDES[side]
        _, dst = halo_refs(r, side)
        return pltpu.make_async_remote_copy(
            dst, dst, halo_send.at[r, side], halo_recv.at[r, side],
            device_id=(gx + dr, gy + dc), device_id_type=MESH)

    def for_sides(do):
        for side in range(8):
            pl.when(there[side])(functools.partial(do, side))

    def pack_borders(r):
        row_out[r, 0] = padded[1, LEFT:LEFT + cols, :]
        row_out[r, 1] = padded[rows, LEFT:LEFT + cols, :]

        def one(i, _):
            col_out[r, 0, pl.ds(i, 1), :] = padded[1 + i, LEFT:LEFT + 1, :]
            col_out[r, 1, pl.ds(i, 1), :] = padded[1 + i, LEFT + cols - 1:LEFT + cols, :]
            return 0

        lax.fori_loop(0, rows, one, 0, unroll=4)
        for n, (dr, dc) in enumerate(SIDES[4:]):
            line = 1 if dr < 0 else rows
            col = LEFT if dc < 0 else LEFT + cols - 1
            corner_out[r, n] = jnp.broadcast_to(padded[line, col:col + 1, :], (8, chan))

    def place_borders(r):
        padded[0, LEFT:LEFT + cols, :] = row_in[r, 0]
        padded[rows + 1, LEFT:LEFT + cols, :] = row_in[r, 1]

        def one(i, _):
            padded[1 + i, LEFT - 1:LEFT, :] = col_in[r, 0, pl.ds(i, 1), :]
            padded[1 + i, LEFT + cols:LEFT + cols + 1, :] = col_in[r, 1, pl.ds(i, 1), :]
            return 0

        lax.fori_loop(0, rows, one, 0, unroll=4)
        for n, (dr, dc) in enumerate(SIDES[4:]):
            line = 0 if dr < 0 else rows + 1
            col = LEFT - 1 if dc < 0 else LEFT + cols
            padded[line, col:col + 1, :] = corner_in[r, n, 0:1, :]

    barrier = pltpu.get_barrier_semaphore()
    count = jnp.int32(1)
    pl.semaphore_signal(barrier, inc=1, device_id=device(at, 1 - core), device_id_type=MESH)
    for dim in "zyx":
        for k in range(1, lengths[dim]):
            pl.semaphore_signal(barrier, inc=1, device_id=device(shifted(dim, k), core), device_id_type=MESH)
            count = count + 1

    def greet(side):
        dr, dc = SIDES[side]
        pl.semaphore_signal(barrier, inc=1, device_id=(gx + dr, gy + dc), device_id_type=MESH)

    for_sides(greet)
    for side in range(8):
        count = count + there[side].astype(jnp.int32)

    load_read = pltpu.make_async_copy(read_ref, weights.at[at["z"], at["y"], at["x"], core], local_sem.at[0])
    load_state = pltpu.make_async_copy(
        state_ref, padded.at[pl.ds(1, rows), pl.ds(LEFT, cols), :], local_sem.at[1])
    load_conv = pltpu.make_async_copy(conv_ref, conv_whole, local_sem.at[2])
    load_read.start()
    load_state.start()
    load_conv.start()

    def clear(side):
        for r in range(ROUNDS):
            _, dst = halo_refs(r, side)
            dst[...] = jnp.zeros(dst.shape, F32)

    for side in range(8):
        pl.when(jnp.logical_not(there[side]))(functools.partial(clear, side))
    load_read.wait()
    load_state.wait()
    pack_borders(0)
    pl.semaphore_wait(barrier, count)

    for_sides(lambda side: halo_copy(0, side).start())
    for order in waves:
        for out, _, _, _ in order[0]:
            out.start()
    own_out.start()

    def next_wave(wave):
        for order in waves:
            for _, arriving, _, _ in order[wave]:
                arriving.wait_recv()
            if wave + 1 < 3:
                for out, _, _, _ in order[wave + 1]:
                    out.start()
            for _, _, on, _ in order[wave]:
                on.start()

    first = lax.broadcasted_iota(jnp.int32, (blocks, blocks), 0)
    second = lax.broadcasted_iota(jnp.int32, (blocks, blocks), 1)
    across = readers_ref[...].astype(F32)
    down = jnp.sum(jnp.where(first == second, across, 0.0), axis=1, keepdims=True)
    same = jnp.where(down == across, 1.0, 0.0)
    slot_across = SLOTS * across + jnp.sum(jnp.where(first < second, same, 0.0), axis=0, keepdims=True)
    slot_down = SLOTS * down + jnp.sum(jnp.where(second < first, same, 0.0), axis=1, keepdims=True)
    slot_at = lax.broadcasted_iota(jnp.int32, (slots, blocks), 0).astype(F32)
    pick[...] = jnp.where(slot_at == slot_across, 1.0, 0.0).astype(BF16)
    slot_at = lax.broadcasted_iota(jnp.int32, (blocks, slots), 1).astype(F32)
    place[...] = jnp.where(slot_at == slot_down, 1.0, 0.0).astype(BF16)

    line = lax.broadcasted_iota(jnp.int32, (16, chan), 0)
    embed = jnp.zeros((16, chan), F32)
    for n, row in enumerate((vector_ref[...], table_ref[1:2, :], table_ref[0:1, :])):
        for m, part in enumerate(split_3(row)):
            embed = jnp.where(line == 3 * n + m, part, embed)
    embed = embed.astype(BF16)
    feature = lax.broadcasted_iota(jnp.int32, (16, cols), 0)

    def split_conv(t, _):
        high, low = split_2(conv_whole[t])
        conv_both[pl.ds(t * chan, chan), 0:chan] = high
        conv_both[pl.ds(t * chan, chan), chan:2 * chan] = low
        return 0

    load_conv.wait()
    lax.fori_loop(0, 9, split_conv, 0)

    def build_cells():
        def one(b, _):
            for i in range(BS):
                for q in range(BS):
                    high, low = split_2(padded[1 + BS * b + i, pl.ds(LEFT + q, block_cols, stride=BS), :])
                    cells[i * BS + q, pl.ds(b * block_cols, block_cols), 0:chan] = high
                    cells[i * BS + q, pl.ds(b * block_cols, block_cols), chan:2 * chan] = low
            return 0

        lax.fori_loop(0, block_rows, one, 0)

        def sort(p, _):
            sorted_cells[p] = jnp.dot(pick[...], cells[p], preferred_element_type=F32)
            return 0

        lax.fori_loop(0, BS * BS, sort, 0)

    def build_taps():
        def one(i, _):
            for s in range(3):
                high, low = split_2(padded[i, LEFT - 1 + s:LEFT - 1 + s + cols, :])
                taps_high[i, :, s * chan:(s + 1) * chan] = high
                taps_low[i, :, s * chan:(s + 1) * chan] = low
            return 0

        lax.fori_loop(0, rows + 2, one, 0, unroll=2)

    def convolve(n):
        def lines(ref):
            parts = [ref[pl.ds(n * STEP + a, STEP)].reshape(STEP * cols, 3 * chan) for a in range(3)]
            return jnp.concatenate(parts, axis=1)

        both = jnp.dot(lines(taps_high), conv_both[...], preferred_element_type=F32)
        low = jnp.dot(lines(taps_low), conv_both[:, 0:chan], preferred_element_type=F32)
        total = both[:, 0:chan] + (both[:, chan:] + low)
        return total.reshape(STEP, cols, chan)

    def convolve_lines(start, stop):
        def one(n, _):
            conv_sum[pl.ds(n * STEP, STEP)] = convolve(n)
            return 0

        lax.fori_loop(start, stop, one, 0)

    def read_out(r):
        def one(k, _):
            c, x = k % 2, k // 2 % nx
            z, y = k // (2 * nx * ny), k // (2 * nx) % ny
            high, low = split_2(weights[z, y, x, c])
            side = jnp.concatenate([high, low], axis=1)
            weight = jnp.concatenate([side, side], axis=0)
            vals = sorted_cells[:, pl.ds(pl.multiple_of(k * SLOTS, SLOTS), SLOTS), :]
            vals = vals.reshape(BS * BS * SLOTS, 2 * chan).astype(BF16)
            both = jnp.dot(vals, weight, preferred_element_type=F32)
            mixed = jnp.tanh(both[:, 0:chan] + both[:, chan:])
            mean = jnp.sum(mixed.reshape(BS * BS, SLOTS, chan), axis=0) * (1.0 / (BS * BS))
            pooled[pl.ds(pl.multiple_of(k * SLOTS, SLOTS), SLOTS), :] = mean
            return 0

        lax.fori_loop(0, nz * ny * nx * 2, one, 0, unroll=4)
        high, low = split_2(pooled[...])
        both = jnp.dot(place[...], jnp.concatenate([high, low], axis=1), preferred_element_type=F32)
        mean = both[:, 0:chan] + both[:, chan:]
        lane = lax.broadcasted_iota(jnp.int32, (block_cols, block_cols), 1)
        deep = lax.broadcasted_iota(jnp.int32, (block_cols, block_cols), 0)
        flags = er_ref[r].astype(F32)
        for b in range(block_rows):
            flag = jnp.sum(jnp.where(lane == deep, flags[b:b + 1, :], 0.0), axis=1, keepdims=True)
            part = jnp.tanh(mean[b * block_cols:(b + 1) * block_cols] + flag * offset_ref[...])
            for q in range(BS):
                spread[b, pl.ds(q, block_cols, stride=BS), :] = part

    def embed_inputs(r):
        wide = jnp.where(
            lax.broadcasted_iota(jnp.int32, (block_cols, cols), 1) // BS
            == lax.broadcasted_iota(jnp.int32, (block_cols, cols), 0), 1.0, 0.0).astype(BF16)
        flag_lanes = jnp.dot(er_ref[r].astype(F32).astype(BF16), wide, preferred_element_type=F32)
        bits_all = syn_ref[r].astype(F32)
        for b in range(block_rows):
            gone = flag_lanes[b:b + 1, :]
            for i in range(b * BS, (b + 1) * BS):
                bits = bits_all[i:i + 1, :]
                one_hot = jnp.where(
                    feature < 3, gone,
                    jnp.where(feature < 6, (1.0 - gone) * bits, (1.0 - gone) * (1.0 - bits))).astype(BF16)
                inputs[r, i] = lax.dot_general(
                    one_hot, embed, (((0,), (0,)), ((), ())), preferred_element_type=F32)

    def updated(r, b, conv):
        old = padded[pl.ds(1 + b * BS, BS), LEFT:LEFT + cols, :]
        return 0.5 * old + jnp.tanh(conv + inputs[r, pl.ds(b * BS, BS)] + spread[b][None])

    def combine(r):
        def one(b, _):
            new = updated(r, b, conv_sum[pl.ds(b * BS, BS)])
            padded[pl.ds(1 + b * BS, BS), LEFT:LEFT + cols, :] = new
            return 0

        lax.fori_loop(0, block_rows, one, 0)

    def store_out(n):
        lines = pl.ds(n * STEP, STEP)
        return pltpu.make_async_copy(conv_sum.at[lines], out_ref.at[lines], local_sem.at[3 + n])

    chunks = rows // STEP

    build_cells()
    for_sides(lambda side: halo_arrival(0, side).wait_recv())
    place_borders(0)
    build_taps()
    next_wave(0)
    convolve_lines(0, chunks)
    next_wave(1)
    embed_inputs(0)
    embed_inputs(1)
    next_wave(2)
    for order in waves:
        for wave in range(3):
            for _, _, _, back in order[wave]:
                back.wait_recv()
    own_in.wait_recv()
    read_out(0)
    combine(0)
    pack_borders(1)
    for_sides(lambda side: halo_copy(1, side).start())
    build_cells()
    read_out(1)
    for_sides(lambda side: halo_arrival(1, side).wait_recv())
    place_borders(1)
    build_taps()
    for n in range(chunks):
        conv_sum[n * STEP:(n + 1) * STEP] = convolve(n)
        for b in range(n * STEP // BS, (n + 1) * STEP // BS):
            conv_sum[b * BS:(b + 1) * BS] = updated(1, b, conv_sum[b * BS:(b + 1) * BS])
        store_out(n).start()

    for order in waves:
        for wave in range(3):
            for out, _, on, _ in order[wave]:
                out.wait_send()
                on.wait_send()
    for n in range(chunks):
        store_out(n).wait()
    own_out.wait_send()
    for r in range(ROUNDS):
        for_sides(lambda side: halo_copy(r, side).wait_send())


def solution(mesh):
    gx_count, gy_count = mesh.shape["gx"], mesh.shape["gy"]
    nx = gy_count // 2
    ny = nx
    nz = gx_count // ny
    copies = max(nz - 1, ny - 1, nx - 1)

    def per_device(state, syndromes, erased, readers, conv, table, vector, read, offset):
        rows, cols, chan = state.shape
        blocks = readers.shape[0]
        slots = gx_count * gy_count * SLOTS
        vmem = pltpu.VMEM
        dma = pltpu.SemaphoreType.DMA
        return pl.pallas_call(
            functools.partial(kernel, (nz, ny, nx)),
            out_shape=jax.ShapeDtypeStruct(state.shape, F32),
            in_specs=[pl.BlockSpec(memory_space=m) for m in (pl.ANY, vmem, vmem, vmem, pl.ANY, vmem, vmem, pl.ANY, vmem)],
            out_specs=pl.BlockSpec(memory_space=pl.ANY),
            scratch_shapes=[
                vmem((nz, ny, nx, 2, chan, chan), F32),
                vmem((rows + 2, cols + 16, chan), F32),
                vmem((rows + 2, cols, 3 * chan), BF16),
                vmem((rows + 2, cols, 3 * chan), BF16),
                vmem((9 * chan, 2 * chan), BF16),
                vmem((rows, cols, chan), F32),
                vmem((BS * BS, blocks, 2 * chan), BF16),
                vmem((BS * BS, slots, 2 * chan), F32),
                vmem((slots, chan), F32),
                vmem((slots, blocks), BF16),
                vmem((blocks, slots), BF16),
                vmem((rows // BS, cols, chan), F32),
                vmem((ROUNDS, 2, cols, chan), F32),
                vmem((ROUNDS, 2, rows, chan), F32),
                vmem((ROUNDS, 2, cols, chan), F32),
                vmem((ROUNDS, 2, rows, chan), F32),
                vmem((ROUNDS, 4, 8, chan), F32),
                vmem((ROUNDS, 4, 8, chan), F32),
                vmem((9, chan, chan), F32),
                vmem((ROUNDS, rows, cols, chan), F32),
                dma((3 + rows // STEP,)),
                dma((3, len(ORDERS), copies)),
                dma((3, len(ORDERS), copies)),
                dma((4, len(ORDERS), copies)),
                dma((4, len(ORDERS), copies)),
                dma((ROUNDS, 8)),
                dma((ROUNDS, 8)),
            ],
            compiler_params=pltpu.CompilerParams(
                collective_id=0, has_side_effects=True, vmem_limit_bytes=56 * 2**20
            ),
        )(state, syndromes, erased, readers.reshape(1, -1), conv, table, vector.reshape(1, -1), read, offset.reshape(1, -1))

    placed = (
        P("gx", "gy", None),
        P(None, "gx", "gy"),
        P(None, "gx", "gy"),
        P(("gx", "gy"), None),
        P(),
        P(),
        P(),
        P(("gx", "gy"), None),
        P(),
    )
    return jax.shard_map(
        per_device, mesh=mesh, in_specs=placed, out_specs=P("gx", "gy", None), check_vma=False
    )
```

```python
import functools

import jax
import jax.numpy as jnp
from jax import lax
from jax.experimental import pallas as pl
from jax.experimental.pallas import tpu as pltpu
from jax.sharding import PartitionSpec as P

MESH = pl.DeviceIdType.MESH
BS = 4
ROUNDS = 2
SLOTS = 8
LEFT = 8
ORDERS = (
    ("z", "y", "x", 0, 40),
    ("z", "x", "y", 40, 80),
    ("x", "z", "y", 80, 104),
    ("y", "z", "x", 104, 128),
)
STEP = 8
SIDES = ((-1, 0), (1, 0), (0, -1), (0, 1), (-1, -1), (-1, 1), (1, -1), (1, 1))
F32 = jnp.float32
BF16 = jnp.bfloat16


def split_2(values):
    high = values.astype(BF16)
    return high, (values - high.astype(F32)).astype(BF16)


def split_3(values):
    high, rest = values.astype(BF16).astype(F32), values
    rest = rest - high
    mid = rest.astype(BF16).astype(F32)
    return high, mid, rest - mid


def kernel(
    sizes,
    state_ref,
    syn_ref,
    er_ref,
    readers_ref,
    conv_ref,
    table_ref,
    vector_ref,
    read_ref,
    offset_ref,
    out_ref,
    weights,
    padded,
    taps_high,
    taps_low,
    conv_both,
    conv_sum,
    cells,
    sorted_cells,
    pooled,
    pick,
    place,
    spread,
    row_out,
    col_out,
    row_in,
    col_in,
    corner_out,
    corner_in,
    conv_whole,
    inputs,
    local_sem,
    send_sem,
    recv_sem,
    core_send,
    core_recv,
    halo_send,
    halo_recv,
):
    nz, ny, nx = sizes
    lengths = {"z": nz, "y": ny, "x": nx}
    rows, cols, chan = conv_sum.shape
    block_rows, block_cols = rows // BS, cols // BS
    blocks = block_rows * block_cols
    slots = nz * ny * nx * 2 * SLOTS
    gx, gy = lax.axis_index("gx"), lax.axis_index("gy")
    at = {"z": gx // ny, "y": gx % ny, "x": gy // 2}
    core = gy % 2
    gx_count, gy_count = nz * ny, nx * 2

    def device(place_of, c):
        return (place_of["z"] * ny + place_of["y"], place_of["x"] * 2 + c)

    def held(order, wave, place_of, c):
        full = order[:wave]
        idx = [pl.ds(0, lengths[d]) if d in full else place_of[d] for d in "zyx"]
        return weights.at[idx[0], idx[1], idx[2], c, pl.ds(order[3], order[4] - order[3]), :]

    def shifted(dim, k):
        moved = dict(at)
        moved[dim] = (at[dim] + k + lengths[dim]) % lengths[dim]
        return moved

    def wave_copies(o, wave):
        made = []
        order = ORDERS[o]
        dim = order[wave]
        for k in range(1, lengths[dim]):
            other, source = shifted(dim, k), shifted(dim, -k)
            mine, theirs = held(order, wave, at, core), held(order, wave, source, core)
            passed = held(order, wave, source, 1 - core)
            made.append(tuple(
                pltpu.make_async_remote_copy(
                    part, part, sems[0].at[wave, o, k - 1], sems[1].at[wave, o, k - 1],
                    device_id=target, device_id_type=MESH)
                for part, sems, target in (
                    (mine, (send_sem, recv_sem), device(other, core)),
                    (theirs, (send_sem, recv_sem), device(other, core)),
                    (theirs, (core_send, core_recv), device(at, 1 - core)),
                    (passed, (core_send, core_recv), device(at, 1 - core)),
                )))
        return made

    def own_pair():
        made = []
        for c in (core, 1 - core):
            part = weights.at[at["z"], at["y"], at["x"], c]
            made.append(pltpu.make_async_remote_copy(
                part, part, core_send.at[3, 0, 0], core_recv.at[3, 0, 0],
                device_id=device(at, 1 - core), device_id_type=MESH))
        return made

    waves = [[wave_copies(o, w) for w in range(3)] for o in range(len(ORDERS))]
    own_out, own_in = own_pair()

    there = []
    for dr, dc in SIDES:
        ok = jnp.bool_(True)
        if dr:
            ok = (gx + dr >= 0) & (gx + dr < gx_count)
        if dc:
            more = (gy + dc >= 0) & (gy + dc < gy_count)
            ok = more if not dr else ok & more
        there.append(ok)

    def halo_refs(r, side):
        dr, dc = SIDES[side]
        if side < 2:
            return row_out.at[r, side], row_in.at[r, side]
        if side < 4:
            return col_out.at[r, side - 2], col_in.at[r, side - 2]
        return corner_out.at[r, side - 4], corner_in.at[r, side - 4]

    opposite = (1, 0, 3, 2, 7, 6, 5, 4)

    def halo_copy(r, side):
        dr, dc = SIDES[side]
        src, _ = halo_refs(r, side)
        _, dst = halo_refs(r, opposite[side])
        return pltpu.make_async_remote_copy(
            src, dst, halo_send.at[r, side], halo_recv.at[r, opposite[side]],
            device_id=(gx + dr, gy + dc), device_id_type=MESH)

    def halo_arrival(r, side):
        dr, dc = SIDES[side]
        _, dst = halo_refs(r, side)
        return pltpu.make_async_remote_copy(
            dst, dst, halo_send.at[r, side], halo_recv.at[r, side],
            device_id=(gx + dr, gy + dc), device_id_type=MESH)

    def for_sides(do):
        for side in range(8):
            pl.when(there[side])(functools.partial(do, side))

    def pack_borders(r):
        row_out[r, 0] = padded[1, LEFT:LEFT + cols, :]
        row_out[r, 1] = padded[rows, LEFT:LEFT + cols, :]

        def one(i, _):
            col_out[r, 0, pl.ds(i, 1), :] = padded[1 + i, LEFT:LEFT + 1, :]
            col_out[r, 1, pl.ds(i, 1), :] = padded[1 + i, LEFT + cols - 1:LEFT + cols, :]
            return 0

        lax.fori_loop(0, rows, one, 0, unroll=4)
        for n, (dr, dc) in enumerate(SIDES[4:]):
            line = 1 if dr < 0 else rows
            col = LEFT if dc < 0 else LEFT + cols - 1
            corner_out[r, n] = jnp.broadcast_to(padded[line, col:col + 1, :], (8, chan))

    def place_borders(r):
        padded[0, LEFT:LEFT + cols, :] = row_in[r, 0]
        padded[rows + 1, LEFT:LEFT + cols, :] = row_in[r, 1]

        def one(i, _):
            padded[1 + i, LEFT - 1:LEFT, :] = col_in[r, 0, pl.ds(i, 1), :]
            padded[1 + i, LEFT + cols:LEFT + cols + 1, :] = col_in[r, 1, pl.ds(i, 1), :]
            return 0

        lax.fori_loop(0, rows, one, 0, unroll=4)
        for n, (dr, dc) in enumerate(SIDES[4:]):
            line = 0 if dr < 0 else rows + 1
            col = LEFT - 1 if dc < 0 else LEFT + cols
            padded[line, col:col + 1, :] = corner_in[r, n, 0:1, :]

    barrier = pltpu.get_barrier_semaphore()
    count = jnp.int32(1)
    pl.semaphore_signal(barrier, inc=1, device_id=device(at, 1 - core), device_id_type=MESH)
    for dim in "zyx":
        for k in range(1, lengths[dim]):
            pl.semaphore_signal(barrier, inc=1, device_id=device(shifted(dim, k), core), device_id_type=MESH)
            count = count + 1

    def greet(side):
        dr, dc = SIDES[side]
        pl.semaphore_signal(barrier, inc=1, device_id=(gx + dr, gy + dc), device_id_type=MESH)

    for_sides(greet)
    for side in range(8):
        count = count + there[side].astype(jnp.int32)

    load_read = pltpu.make_async_copy(read_ref, weights.at[at["z"], at["y"], at["x"], core], local_sem.at[0])
    load_state = pltpu.make_async_copy(
        state_ref, padded.at[pl.ds(1, rows), pl.ds(LEFT, cols), :], local_sem.at[1])
    load_conv = pltpu.make_async_copy(conv_ref, conv_whole, local_sem.at[2])
    load_read.start()
    load_state.start()
    load_conv.start()

    def clear(side):
        for r in range(ROUNDS):
            _, dst = halo_refs(r, side)
            dst[...] = jnp.zeros(dst.shape, F32)

    for side in range(8):
        pl.when(jnp.logical_not(there[side]))(functools.partial(clear, side))
    load_read.wait()
    load_state.wait()
    pack_borders(0)
    pl.semaphore_wait(barrier, count)

    for_sides(lambda side: halo_copy(0, side).start())
    for order in waves:
        for out, _, _, _ in order[0]:
            out.start()
    own_out.start()

    def next_wave(wave):
        for order in waves:
            for _, arriving, _, _ in order[wave]:
                arriving.wait_recv()
            if wave + 1 < 3:
                for out, _, _, _ in order[wave + 1]:
                    out.start()
            for _, _, on, _ in order[wave]:
                on.start()

    first = lax.broadcasted_iota(jnp.int32, (blocks, blocks), 0)
    second = lax.broadcasted_iota(jnp.int32, (blocks, blocks), 1)
    across = readers_ref[...].astype(F32)
    down = jnp.sum(jnp.where(first == second, across, 0.0), axis=1, keepdims=True)
    same = jnp.where(down == across, 1.0, 0.0)
    slot_across = SLOTS * across + jnp.sum(jnp.where(first < second, same, 0.0), axis=0, keepdims=True)
    slot_down = SLOTS * down + jnp.sum(jnp.where(second < first, same, 0.0), axis=1, keepdims=True)
    slot_at = lax.broadcasted_iota(jnp.int32, (slots, blocks), 0).astype(F32)
    pick[...] = jnp.where(slot_at == slot_across, 1.0, 0.0).astype(BF16)
    slot_at = lax.broadcasted_iota(jnp.int32, (blocks, slots), 1).astype(F32)
    place[...] = jnp.where(slot_at == slot_down, 1.0, 0.0).astype(BF16)

    line = lax.broadcasted_iota(jnp.int32, (16, chan), 0)
    embed = jnp.zeros((16, chan), F32)
    for n, row in enumerate((vector_ref[...], table_ref[1:2, :], table_ref[0:1, :])):
        for m, part in enumerate(split_3(row)):
            embed = jnp.where(line == 3 * n + m, part, embed)
    embed = embed.astype(BF16)
    feature = lax.broadcasted_iota(jnp.int32, (16, cols), 0)

    def split_conv(t, _):
        high, low = split_2(conv_whole[t])
        conv_both[pl.ds(t * chan, chan), 0:chan] = high
        conv_both[pl.ds(t * chan, chan), chan:2 * chan] = low
        return 0

    load_conv.wait()
    lax.fori_loop(0, 9, split_conv, 0)

    def build_cells():
        def one(b, _):
            for i in range(BS):
                for q in range(BS):
                    high, low = split_2(padded[1 + BS * b + i, pl.ds(LEFT + q, block_cols, stride=BS), :])
                    cells[i * BS + q, pl.ds(b * block_cols, block_cols), 0:chan] = high
                    cells[i * BS + q, pl.ds(b * block_cols, block_cols), chan:2 * chan] = low
            return 0

        lax.fori_loop(0, block_rows, one, 0, unroll=2)

        def sort(p, _):
            sorted_cells[p] = jnp.dot(pick[...], cells[p], preferred_element_type=F32)
            return 0

        lax.fori_loop(0, BS * BS, sort, 0, unroll=4)

    def build_taps():
        def one(i, _):
            for s in range(3):
                high, low = split_2(padded[i, LEFT - 1 + s:LEFT - 1 + s + cols, :])
                taps_high[i, :, s * chan:(s + 1) * chan] = high
                taps_low[i, :, s * chan:(s + 1) * chan] = low
            return 0

        lax.fori_loop(0, rows + 2, one, 0, unroll=2)

    def convolve(n):
        def lines(ref):
            parts = [ref[pl.ds(n * STEP + a, STEP)].reshape(STEP * cols, 3 * chan) for a in range(3)]
            return jnp.concatenate(parts, axis=1)

        both = jnp.dot(lines(taps_high), conv_both[...], preferred_element_type=F32)
        low = jnp.dot(lines(taps_low), conv_both[:, 0:chan], preferred_element_type=F32)
        total = both[:, 0:chan] + (both[:, chan:] + low)
        return total.reshape(STEP, cols, chan)

    def convolve_lines(start, stop):
        def one(n, _):
            conv_sum[pl.ds(n * STEP, STEP)] = convolve(n)
            return 0

        lax.fori_loop(start, stop, one, 0)

    def read_out(r):
        def one(k, _):
            c, x = k % 2, k // 2 % nx
            z, y = k // (2 * nx * ny), k // (2 * nx) % ny
            high, low = split_2(weights[z, y, x, c])
            side = jnp.concatenate([high, low], axis=1)
            weight = jnp.concatenate([side, side], axis=0)
            vals = sorted_cells[:, pl.ds(pl.multiple_of(k * SLOTS, SLOTS), SLOTS), :]
            vals = vals.reshape(BS * BS * SLOTS, 2 * chan).astype(BF16)
            both = jnp.dot(vals, weight, preferred_element_type=F32)
            mixed = jnp.tanh(both[:, 0:chan] + both[:, chan:])
            mean = jnp.sum(mixed.reshape(BS * BS, SLOTS, chan), axis=0) * (1.0 / (BS * BS))
            pooled[pl.ds(pl.multiple_of(k * SLOTS, SLOTS), SLOTS), :] = mean
            return 0

        lax.fori_loop(0, nz * ny * nx * 2, one, 0, unroll=16)
        high, low = split_2(pooled[...])
        both = jnp.dot(place[...], jnp.concatenate([high, low], axis=1), preferred_element_type=F32)
        mean = both[:, 0:chan] + both[:, chan:]
        lane = lax.broadcasted_iota(jnp.int32, (block_cols, block_cols), 1)
        deep = lax.broadcasted_iota(jnp.int32, (block_cols, block_cols), 0)
        flags = er_ref[r].astype(F32)
        for b in range(block_rows):
            flag = jnp.sum(jnp.where(lane == deep, flags[b:b + 1, :], 0.0), axis=1, keepdims=True)
            part = jnp.tanh(mean[b * block_cols:(b + 1) * block_cols] + flag * offset_ref[...])
            for q in range(BS):
                spread[b, pl.ds(q, block_cols, stride=BS), :] = part

    def embed_inputs(r):
        wide = jnp.where(
            lax.broadcasted_iota(jnp.int32, (block_cols, cols), 1) // BS
            == lax.broadcasted_iota(jnp.int32, (block_cols, cols), 0), 1.0, 0.0).astype(BF16)
        flag_lanes = jnp.dot(er_ref[r].astype(F32).astype(BF16), wide, preferred_element_type=F32)
        bits_all = syn_ref[r].astype(F32)
        for b in range(block_rows):
            gone = flag_lanes[b:b + 1, :]
            for i in range(b * BS, (b + 1) * BS):
                bits = bits_all[i:i + 1, :]
                one_hot = jnp.where(
                    feature < 3, gone,
                    jnp.where(feature < 6, (1.0 - gone) * bits, (1.0 - gone) * (1.0 - bits))).astype(BF16)
                inputs[r, i] = lax.dot_general(
                    one_hot, embed, (((0,), (0,)), ((), ())), preferred_element_type=F32)

    def updated(r, b, conv):
        old = padded[pl.ds(1 + b * BS, BS), LEFT:LEFT + cols, :]
        return 0.5 * old + jnp.tanh(conv + inputs[r, pl.ds(b * BS, BS)] + spread[b][None])

    def combine(r):
        def one(b, _):
            new = updated(r, b, conv_sum[pl.ds(b * BS, BS)])
            padded[pl.ds(1 + b * BS, BS), LEFT:LEFT + cols, :] = new
            return 0

        lax.fori_loop(0, block_rows, one, 0, unroll=2)

    def store_out(n):
        lines = pl.ds(n * STEP, STEP)
        return pltpu.make_async_copy(conv_sum.at[lines], out_ref.at[lines], local_sem.at[3 + n])

    chunks = rows // STEP

    build_cells()
    next_wave(0)
    for_sides(lambda side: halo_arrival(0, side).wait_recv())
    place_borders(0)
    build_taps()
    convolve_lines(0, 2)
    next_wave(1)
    convolve_lines(2, chunks)
    embed_inputs(0)
    embed_inputs(1)
    next_wave(2)
    for order in waves:
        for wave in range(3):
            for _, _, _, back in order[wave]:
                back.wait_recv()
    own_in.wait_recv()
    read_out(0)
    combine(0)
    pack_borders(1)
    for_sides(lambda side: halo_copy(1, side).start())
    build_cells()
    read_out(1)
    for_sides(lambda side: halo_arrival(1, side).wait_recv())
    place_borders(1)
    build_taps()
    for n in range(chunks):
        conv_sum[n * STEP:(n + 1) * STEP] = convolve(n)
        for b in range(n * STEP // BS, (n + 1) * STEP // BS):
            conv_sum[b * BS:(b + 1) * BS] = updated(1, b, conv_sum[b * BS:(b + 1) * BS])
        store_out(n).start()

    for order in waves:
        for wave in range(3):
            for out, _, on, _ in order[wave]:
                out.wait_send()
                on.wait_send()
    for n in range(chunks):
        store_out(n).wait()
    own_out.wait_send()
    for r in range(ROUNDS):
        for_sides(lambda side: halo_copy(r, side).wait_send())


def solution(mesh):
    gx_count, gy_count = mesh.shape["gx"], mesh.shape["gy"]
    nx = gy_count // 2
    ny = nx
    nz = gx_count // ny
    copies = max(nz - 1, ny - 1, nx - 1)

    def per_device(state, syndromes, erased, readers, conv, table, vector, read, offset):
        rows, cols, chan = state.shape
        blocks = readers.shape[0]
        slots = gx_count * gy_count * SLOTS
        vmem = pltpu.VMEM
        dma = pltpu.SemaphoreType.DMA
        return pl.pallas_call(
            functools.partial(kernel, (nz, ny, nx)),
            out_shape=jax.ShapeDtypeStruct(state.shape, F32),
            in_specs=[pl.BlockSpec(memory_space=m) for m in (pl.ANY, vmem, vmem, vmem, pl.ANY, vmem, vmem, pl.ANY, vmem)],
            out_specs=pl.BlockSpec(memory_space=pl.ANY),
            scratch_shapes=[
                vmem((nz, ny, nx, 2, chan, chan), F32),
                vmem((rows + 2, cols + 16, chan), F32),
                vmem((rows + 2, cols, 3 * chan), BF16),
                vmem((rows + 2, cols, 3 * chan), BF16),
                vmem((9 * chan, 2 * chan), BF16),
                vmem((rows, cols, chan), F32),
                vmem((BS * BS, blocks, 2 * chan), BF16),
                vmem((BS * BS, slots, 2 * chan), F32),
                vmem((slots, chan), F32),
                vmem((slots, blocks), BF16),
                vmem((blocks, slots), BF16),
                vmem((rows // BS, cols, chan), F32),
                vmem((ROUNDS, 2, cols, chan), F32),
                vmem((ROUNDS, 2, rows, chan), F32),
                vmem((ROUNDS, 2, cols, chan), F32),
                vmem((ROUNDS, 2, rows, chan), F32),
                vmem((ROUNDS, 4, 8, chan), F32),
                vmem((ROUNDS, 4, 8, chan), F32),
                vmem((9, chan, chan), F32),
                vmem((ROUNDS, rows, cols, chan), F32),
                dma((3 + rows // STEP,)),
                dma((3, len(ORDERS), copies)),
                dma((3, len(ORDERS), copies)),
                dma((4, len(ORDERS), copies)),
                dma((4, len(ORDERS), copies)),
                dma((ROUNDS, 8)),
                dma((ROUNDS, 8)),
            ],
            compiler_params=pltpu.CompilerParams(
                collective_id=0, has_side_effects=True, vmem_limit_bytes=56 * 2**20
            ),
        )(state, syndromes, erased, readers.reshape(1, -1), conv, table, vector.reshape(1, -1), read, offset.reshape(1, -1))

    placed = (
        P("gx", "gy", None),
        P(None, "gx", "gy"),
        P(None, "gx", "gy"),
        P(("gx", "gy"), None),
        P(),
        P(),
        P(),
        P(("gx", "gy"), None),
        P(),
    )
    return jax.shard_map(
        per_device, mesh=mesh, in_specs=placed, out_specs=P("gx", "gy", None), check_vma=False
    )
```
